32 devices in a mesh: dp: 4 (over z), mp: 8 (over y, x, core).
Axes of the slice: x: 2, y: 2, z: 4, core: 2. Of those that a mesh axis runs over, the one named last changes fastest.
Arguments:
- gradient: bfloat16 [4608, 36864], P('dp', 'mp'), may hold values from -14 to 14
- sketches: bfloat16 [1024, 36864], P('dp', 'mp'), may hold values from -4.5 to 4.5
- start_basis: float32 [512, 256], replicated, may hold values from -6 to 6
Outputs:
- preconditioned: bfloat16 [4608, 36864], P('dp', 'mp')
The draws below stay inside these ranges and needn't reach their ends.
All inputs are finite; a program needn't handle non-finite values.
Results may differ from the reference program's by a relative error of at most 0.0065.
Values may be sent and summed in bfloat16 or wider, within the bound.
A program may use at most 128 MiB of HBM per device.

```python
import math
import jax
import jax.numpy as jnp
from jax import lax

D = 4608
FF = 36864
K = 256
ITERS = 4
NS_STEPS = 6
N_DP = 4


def common_rows(key):
    return jnp.clip(jax.random.normal(key, (K, FF), jnp.float32), -5.0, 5.0)


def draw_sketches(key, part):
    base = common_rows(key)
    key = jax.random.fold_in(key, 11)
    first, second = jax.random.split(key)
    count = N_DP * K
    noise = jnp.clip(jax.random.normal(first, (count, FF), jnp.float32), -5.0, 5.0)
    scale = jnp.exp(jax.random.uniform(second, (count, 1), jnp.float32, 0.0, math.log(4.0)))
    shifted = jnp.concatenate([jnp.zeros((1, FF), jnp.float32), noise[:-1]], axis=0)
    mixed = 0.7 * jnp.tile(base, (N_DP, 1)) + noise + 0.6 * shifted
    return (scale * mixed / math.sqrt(FF)).astype(jnp.bfloat16)


def draw_gradient(key, part):
    base = common_rows(key)
    key = jax.random.fold_in(key, 23)
    first = jax.random.fold_in(key, 0)
    repeats = (D + K - 1) // K
    shared = jnp.tile(base, (repeats, 1))[:D]
    noise = jnp.clip(jax.random.normal(first, (D, FF), jnp.float32), -5.0, 5.0)
    return (0.8 * shared + 0.6 * noise).astype(jnp.bfloat16)


def bell_draw(stream_key, dims, spread, bound, kind=jnp.bfloat16):
    return jnp.clip(spread * jax.random.normal(stream_key, dims, jnp.float32), -bound, bound).astype(kind)


def setup_inputs(seed: int = 0) -> dict:
    keys = jax.random.split(jax.random.key(seed), 4)
    return {
        "gradient": draw_gradient(jax.random.fold_in(keys[3], 71), 0),
        "sketches": draw_sketches(jax.random.fold_in(keys[3], 71), 0),
        "start_basis": bell_draw(keys[2], (2 * K, K), 1.0, 6.0, jnp.float32),
    }


def orthonormalize(image):
    scaled = image / jnp.sqrt(jnp.sum(image * image) + 1e-06)
    for inner_step in range(NS_STEPS):
        square = jnp.dot(scaled.T, scaled, precision=lax.Precision.HIGHEST)
        scaled = 1.5 * scaled - 0.5 * jnp.dot(scaled, square, precision=lax.Precision.HIGHEST)
    return scaled

def finish_merge(gram, stacked, start_basis):
    basis = start_basis
    for step in range(ITERS):
        image = jnp.dot(gram, basis, precision=lax.Precision.HIGHEST)
        basis = orthonormalize(image)
    energy = lax.optimization_barrier(jnp.sum(basis * jnp.dot(gram, basis, precision=lax.Precision.HIGHEST), axis=0))
    shrink = 0.5 * jnp.min(energy)
    factor = jnp.sqrt(1.0 - shrink / energy)
    weights = (factor[:, None] * basis.T).astype(jnp.bfloat16)
    return jnp.dot(weights.astype(jnp.float32), stacked.astype(jnp.float32), preferred_element_type=jnp.float32).astype(jnp.bfloat16)

def merge_pair(upper, lower_block, start_basis):
    stacked = jnp.concatenate([upper, lower_block], axis=0)
    gram = jnp.dot(stacked.astype(jnp.float32), stacked.T.astype(jnp.float32), preferred_element_type=jnp.float32)
    return finish_merge(gram, stacked, start_basis)

def apply_sketch(gradient, merged):
    proj = jnp.dot(gradient.astype(jnp.float32), merged.T.astype(jnp.float32), preferred_element_type=jnp.float32)
    sketch_gram = jnp.dot(merged.astype(jnp.float32), merged.T.astype(jnp.float32), preferred_element_type=jnp.float32)
    rho = jnp.trace(sketch_gram) / K
    system = sketch_gram + rho * jnp.eye(K, dtype=jnp.float32)
    lower = jnp.linalg.cholesky(system)
    halfway = lax.linalg.triangular_solve(lower, proj, left_side=False, lower=True, transpose_a=True)
    solved = lax.linalg.triangular_solve(lower, halfway, left_side=False, lower=True, transpose_a=False)
    solved = solved.astype(jnp.bfloat16)
    result = gradient.astype(jnp.float32) - jnp.dot(solved.astype(jnp.float32), merged.astype(jnp.float32), preferred_element_type=jnp.float32)
    return result.astype(jnp.bfloat16)

def reference(gradient, sketches, start_basis):
    blocks = [sketches[i * K:(i + 1) * K] for i in range(N_DP)]
    while len(blocks) > 1:
        blocks = [merge_pair(blocks[2 * j], blocks[2 * j + 1], start_basis) for j in range(len(blocks) // 2)]
    return apply_sketch(gradient, blocks[0])
```

```python
import functools
import jax
import jax.numpy as jnp
from jax import lax
from jax.experimental import pallas as pl
from jax.experimental.pallas import tpu as pltpu
from jax.sharding import PartitionSpec as P

K = 256
ITERS = 4
NS_STEPS = 6
INVERSE_STEPS = 11
BF16 = jnp.bfloat16
F32 = jnp.float32
MESH = pl.DeviceIdType.MESH
VMEM_LIMIT = 56 * 2**20
NN = (((1,), (0,)), ((), ()))
NT = (((1,), (1,)), ((), ()))


def peer(axis, offset):
    size = lax.axis_size(axis)
    return lax.rem(lax.axis_index(axis) + offset, size)


def greet(axes):
    barrier = pltpu.get_barrier_semaphore()
    count = 0
    for axis in axes:
        for offset in range(1, lax.axis_size(axis)):
            pl.semaphore_signal(
                barrier, inc=1, device_id={axis: peer(axis, offset)}, device_id_type=MESH
            )
            count += 1
    pl.semaphore_wait(barrier, count)


def send(axis, offset, source, target, send_sem, recv_sem):
    copy = pltpu.make_async_remote_copy(
        src_ref=source,
        dst_ref=target,
        send_sem=send_sem.at[offset - 1],
        recv_sem=recv_sem.at[offset - 1],
        device_id={axis: peer(axis, offset)},
        device_id_type=MESH,
    )
    copy.start()
    return copy


def rows_of(index, count):
    return pl.ds(pl.multiple_of(index * count, 16), count)


def columns_of(index, count):
    return pl.ds(pl.multiple_of(index * count, 128), count)


def dot(a, b, dims=NN):
    return lax.dot_general(a, b, dims, preferred_element_type=F32)


def split(x):
    high = x.astype(BF16)
    return high, (x - high.astype(F32)).astype(BF16)


def dot_split(a, b, dims=NN):
    return dot(a[0], b[0], dims) + (dot(a[0], b[1], dims) + dot(a[1], b[0], dims))


def sum_slots(ref):
    total = ref[0].astype(F32)
    for slot in range(1, ref.shape[0]):
        total = total + ref[slot].astype(F32)
    return total


def gram_kernel(
    n, mp, width, share, sketch_ref, slice_ref, gram_ref, part, mp_slots, dp_slots,
    local_sem, s0, r0, s1, r1, s2, r2, s3, r3,
):
    me_dp, me_mp = lax.axis_index("dp"), lax.axis_index("mp")
    own = pltpu.make_async_copy(
        sketch_ref.at[:, columns_of(me_dp, width)], slice_ref.at[rows_of(me_dp, K)], local_sem
    )
    own.start()
    greet(("dp", "mp"))
    copies = [
        send(
            "dp", d, sketch_ref.at[:, columns_of(peer("dp", d), width)],
            slice_ref.at[rows_of(me_dp, K)], s0, r0,
        )
        for d in range(1, n)
    ]
    own.wait()
    for copy in copies:
        copy.wait()
    block = 0
    for i in range(n):
        for j in range(i, n):
            part[block * K:(block + 1) * K, :] = dot(
                slice_ref[i * K:(i + 1) * K, :], slice_ref[j * K:(j + 1) * K, :], NT
            ).astype(BF16)
            block += 1
    copies = [
        send("mp", d, part.at[rows_of(peer("mp", d), share)], mp_slots.at[me_mp], s1, r1)
        for d in range(1, mp)
    ]
    mp_slots[me_mp] = part[rows_of(me_mp, share), :]
    for copy in copies:
        copy.wait()
    dp_slots[me_dp] = sum_slots(mp_slots).astype(BF16)
    copies = [
        send("dp", d, dp_slots.at[me_dp], dp_slots.at[me_dp], s2, r2) for d in range(1, n)
    ]
    for copy in copies:
        copy.wait()
    mine = gram_ref.at[rows_of(me_mp, share)]
    mine[...] = sum_slots(dp_slots).astype(BF16)
    copies = [send("mp", d, mine, mine, s3, r3) for d in range(1, mp)]
    for copy in copies:
        copy.wait()


def merge_kernel(n, gram_ref, basis_ref, weights_ref, system_ref, full, following, basis):
    block = 0
    for i in range(n):
        for j in range(i, n):
            value = gram_ref[block * K:(block + 1) * K, :].astype(F32)
            full[i * K:(i + 1) * K, j * K:(j + 1) * K] = value
            if j > i:
                full[j * K:(j + 1) * K, i * K:(i + 1) * K] = value.T
            block += 1
    source, target = full, following
    blocks, first = n, 0
    while blocks > 1:
        pairs = blocks // 2
        sides = [slice(2 * K * p, 2 * K * (p + 1)) for p in range(pairs)]
        for p in range(pairs):
            basis[p] = basis_ref[...]

        def newton_schulz(step, carry):
            for p in range(pairs):
                value = basis[p]
                parts = split(value)
                square = split(dot_split(parts, parts, NT))
                basis[p] = 1.5 * value - 0.5 * dot_split(square, parts)
            return carry

        def iteration(step, carry):
            for p in range(pairs):
                image = dot_split(split(basis[p]), split(source[sides[p], sides[p]]))
                basis[p] = image / jnp.sqrt(jnp.sum(image * image) + 1e-06)
            return lax.fori_loop(0, NS_STEPS, newton_schulz, carry)

        lax.fori_loop(0, ITERS, iteration, 0)
        for p in range(pairs):
            value = basis[p]
            image = dot_split(split(value), split(source[sides[p], sides[p]]))
            energy = jnp.sum(value * image, axis=1, keepdims=True)
            shrink = 0.5 * jnp.min(energy)
            factor = jnp.sqrt(1.0 - shrink / energy)
            weights_ref[first + p] = (factor * value).astype(BF16)
        for a in range(pairs):
            for b in range(a, pairs):
                high, low = split(source[sides[a], sides[b]])
                left = weights_ref[first + a]
                high, low = split(dot(left, high) + dot(left, low))
                right = weights_ref[first + b]
                value = dot(high, right, NT) + dot(low, right, NT)
                target[a * K:(a + 1) * K, b * K:(b + 1) * K] = value
                if b > a:
                    target[b * K:(b + 1) * K, a * K:(a + 1) * K] = value.T
        source, target = target, source
        first += pairs
        blocks = pairs
    system_ref[...] = source[:K, :K]


def invert(system_ref, inverse):
    row = lax.broadcasted_iota(jnp.int32, (K, K), 0)
    column = lax.broadcasted_iota(jnp.int32, (K, K), 1)
    eye = (row == column).astype(F32)
    gram = system_ref[...]
    rho = jnp.sum(gram * eye) / K
    system = gram + rho * eye
    row_sums = jnp.sum(jnp.abs(system), axis=1, keepdims=True)
    bound = jnp.minimum(jnp.max(row_sums), (K + 1) * rho)
    inverse[...] = eye * (2.0 / (bound + rho))
    parts = split(system)

    def step(index, carry):
        value = inverse[...]
        pieces = split(value)
        residual = 2.0 * eye - dot_split(parts, pieces)
        inverse[...] = dot_split(pieces, split(residual))
        return carry

    lax.fori_loop(0, INVERSE_STEPS, step, 0)


def solve_kernel(
    n, mp, width, share, rows, weights_ref, system_ref, slice_ref, gradient_ref,
    merged_ref, solved_ref, grad, level, inverse, proj, sums, mp_slots,
    local_sem, s0, r0, s1, r1, s2, r2,
):
    me_dp, me_mp = lax.axis_index("dp"), lax.axis_index("mp")
    load = pltpu.make_async_copy(gradient_ref, grad, local_sem)
    load.start()
    mine = merged_ref.at[:, columns_of(me_dp, width)]
    source, first, blocks = slice_ref, 0, n
    while blocks > 1:
        blocks //= 2
        for p in range(blocks):
            value = dot(weights_ref[first + p], source[2 * K * p:2 * K * (p + 1), :]).astype(BF16)
            if blocks == 1:
                mine[...] = value
            else:
                level[p * K:(p + 1) * K, :] = value
        source = level
        first += blocks
    greet(("dp", "mp"))
    copies = [send("dp", d, mine, mine, s0, r0) for d in range(1, n)]
    invert(system_ref, inverse)
    load.wait()
    tile = rows // 4

    def multiply(index, start):
        def body(t, carry):
            at = rows_of(t, tile)
            value = dot(
                grad[at, columns_of(index, width)], merged_ref[:, columns_of(index, width)], NT
            )
            sums[at, :] = value if start else sums[at, :] + value
            return carry

        lax.fori_loop(0, 4, body, 0)

    multiply(me_dp, True)
    for d in range(1, n):
        copies[d - 1].wait()
        multiply(peer("dp", n - d), False)
    proj[:rows, :] = sums[...].astype(BF16)
    if share * mp > rows:
        proj[rows:, :] = jnp.zeros((share * mp - rows, K), BF16)
    copies = [
        send("mp", d, proj.at[rows_of(peer("mp", d), share)], mp_slots.at[me_mp], s1, r1)
        for d in range(1, mp)
    ]
    mp_slots[me_mp] = proj[rows_of(me_mp, share), :]
    for copy in copies:
        copy.wait()
    solved = dot_split(split(sum_slots(mp_slots)), split(inverse[...]))
    part = solved_ref.at[rows_of(me_mp, share)]
    part[...] = solved.astype(BF16)
    copies = [send("mp", d, part, part, s2, r2) for d in range(1, mp)]
    for copy in copies:
        copy.wait()


def vmem():
    return pl.BlockSpec(memory_space=pltpu.VMEM)


def anywhere():
    return pl.BlockSpec(memory_space=pl.ANY)


def dma(count):
    return pltpu.SemaphoreType.DMA((count,))


def round_up(value, multiple):
    return -(-value // multiple) * multiple


def local(gradient, sketches, start_basis):
    n, mp = lax.axis_size("dp"), lax.axis_size("mp")
    rows, columns = gradient.shape
    width = round_up(-(-columns // n), 128)
    padding = ((0, 0), (0, width * n - columns))
    wide_gradient, wide_sketches = gradient, sketches
    if width * n > columns:
        wide_gradient, wide_sketches = jnp.pad(gradient, padding), jnp.pad(sketches, padding)

    gram_rows = n * (n + 1) // 2 * K
    share = round_up(-(-gram_rows // mp), 16)
    gram_rows = share * mp
    slices, gram = pl.pallas_call(
        functools.partial(gram_kernel, n, mp, width, share),
        out_shape=[
            jax.ShapeDtypeStruct((n * K, width), BF16),
            jax.ShapeDtypeStruct((gram_rows, K), BF16),
        ],
        in_specs=[anywhere()],
        out_specs=[vmem(), vmem()],
        scratch_shapes=[
            pltpu.VMEM((gram_rows, K), BF16),
            pltpu.VMEM((mp, share, K), BF16),
            pltpu.VMEM((n, share, K), BF16),
            pltpu.SemaphoreType.DMA,
            dma(n - 1), dma(n - 1), dma(mp - 1), dma(mp - 1),
            dma(n - 1), dma(n - 1), dma(mp - 1), dma(mp - 1),
        ],
        compiler_params=pltpu.CompilerParams(
            collective_id=0, has_side_effects=True, vmem_limit_bytes=VMEM_LIMIT
        ),
        name="gram",
    )(wide_sketches)

    weights, system = pl.pallas_call(
        functools.partial(merge_kernel, n),
        out_shape=[
            jax.ShapeDtypeStruct((n - 1, K, 2 * K), BF16),
            jax.ShapeDtypeStruct((K, K), F32),
        ],
        in_specs=[vmem(), vmem()],
        out_specs=[vmem(), vmem()],
        scratch_shapes=[
            pltpu.VMEM((n * K, n * K), F32),
            pltpu.VMEM((n * K // 2, n * K // 2), F32),
            pltpu.VMEM((n // 2, K, 2 * K), F32),
        ],
        compiler_params=pltpu.CompilerParams(vmem_limit_bytes=VMEM_LIMIT),
        name="merge",
    )(gram, start_basis.T)

    share = round_up(-(-rows // mp), 16)
    merged, solved = pl.pallas_call(
        functools.partial(solve_kernel, n, mp, width, share, rows),
        out_shape=[
            jax.ShapeDtypeStruct((K, n * width), BF16),
            jax.ShapeDtypeStruct((share * mp, K), BF16),
        ],
        in_specs=[vmem(), vmem(), vmem(), anywhere()],
        out_specs=[vmem(), vmem()],
        scratch_shapes=[
            pltpu.VMEM((rows, n * width), BF16),
            pltpu.VMEM((n // 2 * K, width), BF16),
            pltpu.VMEM((K, K), F32),
            pltpu.VMEM((share * mp, K), BF16),
            pltpu.VMEM((rows, K), F32),
            pltpu.VMEM((mp, share, K), BF16),
            pltpu.SemaphoreType.DMA,
            dma(n - 1), dma(n - 1), dma(mp - 1), dma(mp - 1), dma(mp - 1), dma(mp - 1),
        ],
        compiler_params=pltpu.CompilerParams(
            collective_id=1, has_side_effects=True, vmem_limit_bytes=VMEM_LIMIT
        ),
        name="solve",
    )(weights, system, slices, wide_gradient)
    result = gradient.astype(F32) - jnp.dot(
        solved[:rows], merged[:, :columns], preferred_element_type=F32
    )
    return result.astype(BF16)


def solution(mesh):
    in_specs = (P("dp", "mp"), P("dp", "mp"), P())
    out_specs = P("dp", "mp")
    return jax.shard_map(local, mesh=mesh, in_specs=in_specs, out_specs=out_specs, check_vma=False)
```

```python
import functools
import jax
import jax.numpy as jnp
from jax import lax
from jax.experimental import pallas as pl
from jax.experimental.pallas import tpu as pltpu
from jax.sharding import PartitionSpec as P

K = 256
ITERS = 4
NS_STEPS = 6
INVERSE_STEPS = 11
BF16 = jnp.bfloat16
F32 = jnp.float32
MESH = pl.DeviceIdType.MESH
MIB = 2**20
NN = (((1,), (0,)), ((), ()))
NT = (((1,), (1,)), ((), ()))


def peer(axis, offset):
    size = lax.axis_size(axis)
    return lax.rem(lax.axis_index(axis) + offset, size)


def greet(axes):
    barrier = pltpu.get_barrier_semaphore()
    count = 0
    for axis in axes:
        for offset in range(1, lax.axis_size(axis)):
            pl.semaphore_signal(
                barrier, inc=1, device_id={axis: peer(axis, offset)}, device_id_type=MESH
            )
            count += 1
    pl.semaphore_wait(barrier, count)


def send(axis, offset, source, target, send_sem, recv_sem):
    copy = pltpu.make_async_remote_copy(
        src_ref=source,
        dst_ref=target,
        send_sem=send_sem.at[offset - 1],
        recv_sem=recv_sem.at[offset - 1],
        device_id={axis: peer(axis, offset)},
        device_id_type=MESH,
    )
    copy.start()
    return copy


def core_send(source, target, core, chip, send_sem, recv_sem):
    copy = pltpu.make_async_remote_copy(
        src_ref=source,
        dst_ref=target,
        send_sem=send_sem,
        recv_sem=recv_sem,
        device_id={"mp": 2 * chip + 1 - core},
        device_id_type=MESH,
    )
    copy.start()
    return copy


def chip_send(offset, source, target, core, chip, send_sem, recv_sem):
    chips = lax.axis_size("mp") // 2
    copy = pltpu.make_async_remote_copy(
        src_ref=source,
        dst_ref=target,
        send_sem=send_sem.at[offset - 1],
        recv_sem=recv_sem.at[offset - 1],
        device_id={"mp": 2 * lax.rem(chip + offset, chips) + core},
        device_id_type=MESH,
    )
    copy.start()
    return copy


def rows_of(index, count):
    return pl.ds(pl.multiple_of(index * count, 16), count)


def columns_of(index, count):
    return pl.ds(pl.multiple_of(index * count, 128), count)


def dot(a, b, dims=NN):
    return lax.dot_general(a, b, dims, preferred_element_type=F32)


def split(x):
    high = x.astype(BF16)
    return high, (x - high.astype(F32)).astype(BF16)


def dot_split(a, b, dims=NN):
    return dot(a[0], b[0], dims) + (dot(a[0], b[1], dims) + dot(a[1], b[0], dims))


def sum_slots(ref):
    total = ref[0].astype(F32)
    for slot in range(1, ref.shape[0]):
        total = total + ref[slot].astype(F32)
    return total


def gram_kernel(
    n, mp, width, share, sketch_ref, basis_ref, slice_ref, gram_ref, turned_ref,
    part, core_slot, half, mp_slots, dp_slots,
    local_sem, s0, r0, s1, r1, s2, r2, s3, r3, s4, r4, s5, r5,
):
    me_dp, me_mp = lax.axis_index("dp"), lax.axis_index("mp")
    own = pltpu.make_async_copy(
        sketch_ref.at[:, columns_of(me_dp, width)], slice_ref.at[rows_of(me_dp, K)], local_sem
    )
    own.start()
    greet(("dp", "mp"))
    copies = [
        send(
            "dp", d, sketch_ref.at[:, columns_of(peer("dp", d), width)],
            slice_ref.at[rows_of(me_dp, K)], s0, r0,
        )
        for d in range(1, n)
    ]
    turned_ref[...] = basis_ref[...].T
    own.wait()
    for copy in copies:
        copy.wait()
    block = 0
    for i in range(n):
        for j in range(i, n):
            part[block * K:(block + 1) * K, :] = dot(
                slice_ref[i * K:(i + 1) * K, :], slice_ref[j * K:(j + 1) * K, :], NT
            ).astype(BF16)
            block += 1
    chips = mp // 2
    core, chip = lax.rem(me_mp, 2), me_mp // 2
    twin = 1 - core
    copy = core_send(part.at[rows_of(twin, chips * share)], core_slot, core, chip, s1, r1)
    copy.wait()
    half[...] = (
        part[rows_of(core, chips * share), :].astype(F32) + core_slot[...].astype(F32)
    ).astype(BF16)
    copies = [
        chip_send(d, half.at[rows_of(lax.rem(chip + d, chips), share)], mp_slots.at[chip], core, chip, s2, r2)
        for d in range(1, chips)
    ]
    mp_slots[chip] = half[rows_of(chip, share), :]
    for copy in copies:
        copy.wait()
    dp_slots[me_dp] = sum_slots(mp_slots).astype(BF16)
    copies = [
        send("dp", d, dp_slots.at[me_dp], dp_slots.at[me_dp], s3, r3) for d in range(1, n)
    ]
    for copy in copies:
        copy.wait()
    mine = gram_ref.at[rows_of(core * chips + chip, share)]
    mine[...] = sum_slots(dp_slots).astype(BF16)
    copies = [chip_send(d, mine, mine, core, chip, s4, r4) for d in range(1, chips)]
    for copy in copies:
        copy.wait()
    mine = gram_ref.at[rows_of(core, chips * share)]
    copy = core_send(mine, mine, core, chip, s5, r5)
    copy.wait()


def merge_kernel(n, gram_ref, basis_ref, weights_ref, system_ref, full, following, basis, fine):
    block = 0
    for i in range(n):
        for j in range(i, n):
            value = gram_ref[block * K:(block + 1) * K, :].astype(F32)
            full[i * K:(i + 1) * K, j * K:(j + 1) * K] = value
            if j > i:
                full[j * K:(j + 1) * K, i * K:(i + 1) * K] = value.T
            block += 1
    source, target = full, following
    blocks, first = n, 0
    while blocks > 1:
        pairs = blocks // 2
        sides = [slice(2 * K * p, 2 * K * (p + 1)) for p in range(pairs)]
        for p in range(pairs):
            basis[p] = basis_ref[...]
            fine[2 * p], fine[2 * p + 1] = split(source[sides[p], sides[p]])

        def multiply(value, p):
            high, low = split(value)
            image = dot(high, fine[2 * p]) + dot(low, fine[2 * p])
            if blocks == n:
                return image
            return image + dot(high, fine[2 * p + 1])

        def newton_schulz(step, carry):
            for p in range(pairs):
                value = basis[p]
                short = value.astype(BF16)
                square = dot(short, short, NT).astype(BF16)
                basis[p] = 1.5 * value - 0.5 * dot(square, short)
            return carry

        def iteration(step, carry):
            for p in range(pairs):
                image = multiply(basis[p], p)
                basis[p] = image / jnp.sqrt(jnp.sum(image * image) + 1e-06)
            return lax.fori_loop(0, NS_STEPS, newton_schulz, carry)

        lax.fori_loop(0, ITERS, iteration, 0)
        for p in range(pairs):
            value = basis[p]
            image = multiply(value, p)
            energy = jnp.sum(value * image, axis=1, keepdims=True)
            shrink = 0.5 * jnp.min(energy)
            factor = jnp.sqrt(1.0 - shrink / energy)
            weights_ref[first + p] = (factor * value).astype(BF16)
        for a in range(pairs):
            for b in range(a, pairs):
                high, low = split(source[sides[a], sides[b]])
                left = weights_ref[first + a]
                high, low = split(dot(left, high) + dot(left, low))
                right = weights_ref[first + b]
                value = dot(high, right, NT) + dot(low, right, NT)
                target[a * K:(a + 1) * K, b * K:(b + 1) * K] = value
                if b > a:
                    target[b * K:(b + 1) * K, a * K:(a + 1) * K] = value.T
        source, target = target, source
        first += pairs
        blocks = pairs
    system_ref[...] = source[:K, :K]


def invert(system_ref, inverse):
    row = lax.broadcasted_iota(jnp.int32, (K, K), 0)
    column = lax.broadcasted_iota(jnp.int32, (K, K), 1)
    eye = (row == column).astype(F32)
    gram = system_ref[...]
    rho = jnp.sum(gram * eye) / K
    system = gram + rho * eye
    row_sums = jnp.sum(jnp.abs(system), axis=1, keepdims=True)
    bound = jnp.minimum(jnp.max(row_sums), (K + 1) * rho)
    inverse[...] = eye * (2.0 / (bound + rho))
    parts = split(system)

    def step(index, carry):
        value = inverse[...]
        pieces = split(value)
        residual = 2.0 * eye - dot_split(parts, pieces)
        inverse[...] = dot_split(pieces, split(residual))
        return carry

    lax.fori_loop(0, INVERSE_STEPS, step, 0)


def solve_kernel(
    n, mp, width, share, rows, weights_ref, system_ref, slice_ref, gradient_ref,
    merged_ref, solved_ref, grad, level, inverse, proj, sums, mp_slots,
    local_sem, s0, r0, s1, r1, s2, r2, s3, r3,
):
    me_dp, me_mp = lax.axis_index("dp"), lax.axis_index("mp")
    load = pltpu.make_async_copy(gradient_ref, grad, local_sem)
    load.start()
    mine = merged_ref.at[:, columns_of(me_dp, width)]
    source, first, blocks = slice_ref, 0, n
    while blocks > 1:
        blocks //= 2
        for p in range(blocks):
            value = dot(weights_ref[first + p], source[2 * K * p:2 * K * (p + 1), :]).astype(BF16)
            if blocks == 1:
                mine[...] = value
            else:
                level[p * K:(p + 1) * K, :] = value
        source = level
        first += blocks
    greet(("dp", "mp"))
    def pass_on(index, offset, semaphores):
        part = merged_ref.at[:, columns_of(index, width)]
        at = lax.rem(index + n, n)
        return pltpu.make_async_remote_copy(
            src_ref=part,
            dst_ref=part,
            send_sem=semaphores[0].at[at],
            recv_sem=semaphores[1].at[at],
            device_id={"dp": lax.rem(me_dp + offset + n, n)},
            device_id_type=MESH,
        )

    up, down = (s0, r0), (s3, r3)

    @pl.when(me_dp < n - 1)
    def _():
        pass_on(me_dp, 1, up).start()

    @pl.when(me_dp > 0)
    def _():
        pass_on(me_dp, -1, down).start()

    invert(system_ref, inverse)
    load.wait()
    tile = rows // 4

    def multiply(index, start):
        def body(t, carry):
            at = rows_of(t, tile)
            value = dot(
                grad[at, columns_of(index, width)], merged_ref[:, columns_of(index, width)], NT
            )
            sums[at, :] = value if start else sums[at, :] + value
            return carry

        lax.fori_loop(0, 4, body, 0)

    multiply(me_dp, True)
    for d in range(1, n):
        below, above = me_dp - d, me_dp + d

        @pl.when(below >= 0)
        def _():
            pass_on(below, 1, up).wait_recv()

        @pl.when((below >= 0) & (me_dp < n - 1))
        def _():
            pass_on(below, 1, up).start()

        @pl.when(above < n)
        def _():
            pass_on(above, -1, down).wait_recv()

        @pl.when((above < n) & (me_dp > 0))
        def _():
            pass_on(above, -1, down).start()

        @pl.when(below >= 0)
        def _():
            multiply(below, False)

        @pl.when(above < n)
        def _():
            multiply(above, False)

    for d in range(n):

        @pl.when((me_dp - d >= 0) & (me_dp < n - 1))
        def _():
            pass_on(me_dp - d, 1, up).wait_send()

        @pl.when((me_dp + d < n) & (me_dp > 0))
        def _():
            pass_on(me_dp + d, -1, down).wait_send()

    proj[:rows, :] = sums[...].astype(BF16)
    if share * mp > rows:
        proj[rows:, :] = jnp.zeros((share * mp - rows, K), BF16)
    copies = [
        send("mp", d, proj.at[rows_of(peer("mp", d), share)], mp_slots.at[me_mp], s1, r1)
        for d in range(1, mp)
    ]
    mp_slots[me_mp] = proj[rows_of(me_mp, share), :]
    for copy in copies:
        copy.wait()
    solved = dot_split(split(sum_slots(mp_slots)), split(inverse[...]))
    part = solved_ref.at[rows_of(me_mp, share)]
    part[...] = solved.astype(BF16)
    copies = [send("mp", d, part, part, s2, r2) for d in range(1, mp)]
    for copy in copies:
        copy.wait()


def subtract_kernel(gradient_ref, solved_ref, merged_ref, result_ref):
    result = gradient_ref[...].astype(F32) - dot(solved_ref[...], merged_ref[...])
    result_ref[...] = result.astype(BF16)


def vmem():
    return pl.BlockSpec(memory_space=pltpu.VMEM)


def anywhere():
    return pl.BlockSpec(memory_space=pl.ANY)


def dma(count):
    return pltpu.SemaphoreType.DMA((count,))


def round_up(value, multiple):
    return -(-value // multiple) * multiple


def local(gradient, sketches, start_basis):
    n, mp = lax.axis_size("dp"), lax.axis_size("mp")
    rows, columns = gradient.shape
    width = round_up(-(-columns // n), 128)
    padding = ((0, 0), (0, width * n - columns))
    wide_gradient, wide_sketches = gradient, sketches
    if width * n > columns:
        wide_gradient, wide_sketches = jnp.pad(gradient, padding), jnp.pad(sketches, padding)

    gram_rows = n * (n + 1) // 2 * K
    share = round_up(-(-gram_rows // mp), 16)
    gram_rows = share * mp
    one = pltpu.SemaphoreType.DMA
    slices, gram, turned = pl.pallas_call(
        functools.partial(gram_kernel, n, mp, width, share),
        out_shape=[
            jax.ShapeDtypeStruct((n * K, width), BF16),
            jax.ShapeDtypeStruct((gram_rows, K), BF16),
            jax.ShapeDtypeStruct((K, 2 * K), F32),
        ],
        in_specs=[anywhere(), vmem()],
        out_specs=[vmem(), vmem(), vmem()],
        scratch_shapes=[
            pltpu.VMEM((gram_rows, K), BF16),
            pltpu.VMEM((gram_rows // 2, K), BF16),
            pltpu.VMEM((gram_rows // 2, K), BF16),
            pltpu.VMEM((mp // 2, share, K), BF16),
            pltpu.VMEM((n, share, K), BF16),
            one, dma(n - 1), dma(n - 1), one, one, dma(mp // 2 - 1), dma(mp // 2 - 1),
            dma(n - 1), dma(n - 1), dma(mp // 2 - 1), dma(mp // 2 - 1), one, one,
        ],
        compiler_params=pltpu.CompilerParams(
            collective_id=0, has_side_effects=True, vmem_limit_bytes=MIB * 16 + 8 * gram_rows * K
        ),
        name="gram",
    )(wide_sketches, start_basis)

    weights, system = pl.pallas_call(
        functools.partial(merge_kernel, n),
        out_shape=[
            jax.ShapeDtypeStruct((n - 1, K, 2 * K), BF16),
            jax.ShapeDtypeStruct((K, K), F32),
        ],
        in_specs=[vmem(), vmem()],
        out_specs=[vmem(), vmem()],
        scratch_shapes=[
            pltpu.VMEM((n * K, n * K), F32),
            pltpu.VMEM((n * K // 2, n * K // 2), F32),
            pltpu.VMEM((n // 2, K, 2 * K), F32),
            pltpu.VMEM((n, 2 * K, 2 * K), BF16),
        ],
        compiler_params=pltpu.CompilerParams(vmem_limit_bytes=MIB * 16 + 8 * (n * K) ** 2),
        name="merge",
    )(gram, turned)

    share = round_up(-(-rows // mp), 16)
    merged, solved = pl.pallas_call(
        functools.partial(solve_kernel, n, mp, width, share, rows),
        out_shape=[
            jax.ShapeDtypeStruct((K, n * width), BF16),
            jax.ShapeDtypeStruct((share * mp, K), BF16),
        ],
        in_specs=[vmem(), vmem(), vmem(), anywhere()],
        out_specs=[vmem(), vmem()],
        scratch_shapes=[
            pltpu.VMEM((rows, n * width), BF16),
            pltpu.VMEM((n // 2 * K, width), BF16),
            pltpu.VMEM((K, K), F32),
            pltpu.VMEM((share * mp, K), BF16),
            pltpu.VMEM((rows, K), F32),
            pltpu.VMEM((mp, share, K), BF16),
            one, dma(n), dma(n), dma(mp - 1), dma(mp - 1), dma(mp - 1), dma(mp - 1), dma(n), dma(n),
        ],
        compiler_params=pltpu.CompilerParams(
            collective_id=1, has_side_effects=True, vmem_limit_bytes=MIB * 20 + 2 * rows * n * width
        ),
        name="solve",
    )(weights, system, slices, wide_gradient)
    tile = rows // 8 if rows % 128 == 0 else rows
    return pl.pallas_call(
        subtract_kernel,
        out_shape=jax.ShapeDtypeStruct((rows, columns), BF16),
        grid=(rows // tile,),
        in_specs=[
            pl.BlockSpec((tile, columns), lambda i: (i, 0)),
            pl.BlockSpec((tile, K), lambda i: (i, 0)),
            pl.BlockSpec((K, columns), lambda i: (0, 0)),
        ],
        out_specs=pl.BlockSpec((tile, columns), lambda i: (i, 0)),
        compiler_params=pltpu.CompilerParams(vmem_limit_bytes=MIB * 24),
        name="subtract",
    )(gradient, solved[:rows], merged[:, :columns])


def solution(mesh):
    in_specs = (P("dp", "mp"), P("dp", "mp"), P())
    out_specs = P("dp", "mp")
    return jax.shard_map(local, mesh=mesh, in_specs=in_specs, out_specs=out_specs, check_vma=False)
```

```python
import functools
import jax
import jax.numpy as jnp
from jax import lax
from jax.experimental import pallas as pl
from jax.experimental.pallas import tpu as pltpu
from jax.sharding import PartitionSpec as P

K = 256
ITERS = 4
NS_STEPS = 6
INVERSE_STEPS = 11
BF16 = jnp.bfloat16
F32 = jnp.float32
MESH = pl.DeviceIdType.MESH
MIB = 2**20
NN = (((1,), (0,)), ((), ()))
NT = (((1,), (1,)), ((), ()))


def peer(axis, offset):
    size = lax.axis_size(axis)
    return lax.rem(lax.axis_index(axis) + offset, size)


def greet(axes):
    barrier = pltpu.get_barrier_semaphore()
    count = 0
    for axis in axes:
        for offset in range(1, lax.axis_size(axis)):
            pl.semaphore_signal(
                barrier, inc=1, device_id={axis: peer(axis, offset)}, device_id_type=MESH
            )
            count += 1
    pl.semaphore_wait(barrier, count)


def send(axis, offset, source, target, send_sem, recv_sem):
    copy = pltpu.make_async_remote_copy(
        src_ref=source,
        dst_ref=target,
        send_sem=send_sem.at[offset - 1],
        recv_sem=recv_sem.at[offset - 1],
        device_id={axis: peer(axis, offset)},
        device_id_type=MESH,
    )
    copy.start()
    return copy


def core_send(source, target, core, chip, send_sem, recv_sem):
    copy = pltpu.make_async_remote_copy(
        src_ref=source,
        dst_ref=target,
        send_sem=send_sem,
        recv_sem=recv_sem,
        device_id={"mp": 2 * chip + 1 - core},
        device_id_type=MESH,
    )
    copy.start()
    return copy


def chip_send(offset, source, target, core, chip, send_sem, recv_sem):
    chips = lax.axis_size("mp") // 2
    copy = pltpu.make_async_remote_copy(
        src_ref=source,
        dst_ref=target,
        send_sem=send_sem.at[offset - 1],
        recv_sem=recv_sem.at[offset - 1],
        device_id={"mp": 2 * lax.rem(chip + offset, chips) + core},
        device_id_type=MESH,
    )
    copy.start()
    return copy


def rows_of(index, count):
    return pl.ds(pl.multiple_of(index * count, 16), count)


def columns_of(index, count):
    return pl.ds(pl.multiple_of(index * count, 128), count)


def dot(a, b, dims=NN):
    return lax.dot_general(a, b, dims, preferred_element_type=F32)


def split(x):
    high = x.astype(BF16)
    return high, (x - high.astype(F32)).astype(BF16)


def dot_split(a, b, dims=NN):
    return dot(a[0], b[0], dims) + (dot(a[0], b[1], dims) + dot(a[1], b[0], dims))


def sum_slots(ref):
    total = ref[0].astype(F32)
    for slot in range(1, ref.shape[0]):
        total = total + ref[slot].astype(F32)
    return total


def gram_kernel(
    n, mp, width, share, sketch_ref, basis_ref, slice_ref, gram_ref, turned_ref,
    part, core_slot, half, mp_slots, plane, dp_slots,
    local_sem, s0, r0, s1, r1, s2, r2, s3, r3, s4, r4, s5, r5, s6, r6,
):
    me_dp, me_mp = lax.axis_index("dp"), lax.axis_index("mp")
    own = pltpu.make_async_copy(
        sketch_ref.at[:, columns_of(me_dp, width)], slice_ref.at[rows_of(me_dp, K)], local_sem
    )
    own.start()
    greet(("dp", "mp"))
    copies = [
        send(
            "dp", d, sketch_ref.at[:, columns_of(peer("dp", d), width)],
            slice_ref.at[rows_of(me_dp, K)], s0, r0,
        )
        for d in range(1, n)
    ]
    turned_ref[...] = basis_ref[...].T
    own.wait()
    for copy in copies:
        copy.wait()
    block = 0
    for i in range(n):
        for j in range(i, n):
            part[block * K:(block + 1) * K, :] = dot(
                slice_ref[i * K:(i + 1) * K, :], slice_ref[j * K:(j + 1) * K, :], NT
            ).astype(BF16)
            block += 1
    chips = mp // 2
    core, chip = lax.rem(me_mp, 2), me_mp // 2
    twin = 1 - core
    copy = core_send(part.at[rows_of(twin, chips * share)], core_slot, core, chip, s1, r1)
    copy.wait()
    half[...] = (
        part[rows_of(core, chips * share), :].astype(F32) + core_slot[...].astype(F32)
    ).astype(BF16)
    copies = [
        chip_send(d, half.at[rows_of(lax.rem(chip + d, chips), share)], mp_slots.at[chip], core, chip, s2, r2)
        for d in range(1, chips)
    ]
    mp_slots[chip] = half[rows_of(chip, share), :]
    for copy in copies:
        copy.wait()
    plane[...] = sum_slots(mp_slots).astype(BF16)
    fourth = share // n
    copies = [
        send("dp", d, plane.at[rows_of(peer("dp", d), fourth)], dp_slots.at[me_dp], s3, r3)
        for d in range(1, n)
    ]
    dp_slots[me_dp] = plane[rows_of(me_dp, fourth), :]
    for copy in copies:
        copy.wait()
    mine = gram_ref.at[rows_of((core * chips + chip) * n + me_dp, fourth)]
    mine[...] = sum_slots(dp_slots).astype(BF16)
    copies = [send("dp", d, mine, mine, s6, r6) for d in range(1, n)]
    for copy in copies:
        copy.wait()
    mine = gram_ref.at[rows_of(core * chips + chip, share)]
    copies = [chip_send(d, mine, mine, core, chip, s4, r4) for d in range(1, chips)]
    for copy in copies:
        copy.wait()
    mine = gram_ref.at[rows_of(core, chips * share)]
    copy = core_send(mine, mine, core, chip, s5, r5)
    copy.wait()


def merge_kernel(n, gram_ref, basis_ref, weights_ref, system_ref, full, following, basis, fine):
    block = 0
    for i in range(n):
        for j in range(i, n):
            value = gram_ref[block * K:(block + 1) * K, :].astype(F32)
            full[i * K:(i + 1) * K, j * K:(j + 1) * K] = value
            if j > i:
                full[j * K:(j + 1) * K, i * K:(i + 1) * K] = value.T
            block += 1
    source, target = full, following
    blocks, first = n, 0
    while blocks > 1:
        pairs = blocks // 2
        sides = [slice(2 * K * p, 2 * K * (p + 1)) for p in range(pairs)]
        for p in range(pairs):
            basis[p] = basis_ref[...]
            fine[2 * p], fine[2 * p + 1] = split(source[sides[p], sides[p]])

        def multiply(value, p):
            high, low = split(value)
            image = dot(high, fine[2 * p]) + dot(low, fine[2 * p])
            if blocks == n:
                return image
            return image + dot(high, fine[2 * p + 1])

        def newton_schulz(step, carry):
            for p in range(pairs):
                value = basis[p]
                short = value.astype(BF16)
                square = dot(short, short, NT).astype(BF16)
                basis[p] = 1.5 * value - 0.5 * dot(square, short)
            return carry

        def iteration(step, carry):
            for p in range(pairs):
                image = multiply(basis[p], p)
                basis[p] = image / jnp.sqrt(jnp.sum(image * image) + 1e-06)
            return lax.fori_loop(0, NS_STEPS, newton_schulz, carry, unroll=True)

        lax.fori_loop(0, ITERS, iteration, 0)
        for p in range(pairs):
            value = basis[p]
            image = multiply(value, p)
            energy = jnp.sum(value * image, axis=1, keepdims=True)
            shrink = 0.5 * jnp.min(energy)
            factor = jnp.sqrt(1.0 - shrink / energy)
            weights_ref[first + p] = (factor * value).astype(BF16)
        for a in range(pairs):
            for b in range(a, pairs):
                high, low = split(source[sides[a], sides[b]])
                left = weights_ref[first + a]
                high, low = split(dot(left, high) + dot(left, low))
                right = weights_ref[first + b]
                value = dot(high, right, NT) + dot(low, right, NT)
                target[a * K:(a + 1) * K, b * K:(b + 1) * K] = value
                if b > a:
                    target[b * K:(b + 1) * K, a * K:(a + 1) * K] = value.T
        source, target = target, source
        first += pairs
        blocks = pairs
    system_ref[...] = source[:K, :K]


def invert(system_ref, inverse):
    row = lax.broadcasted_iota(jnp.int32, (K, K), 0)
    column = lax.broadcasted_iota(jnp.int32, (K, K), 1)
    eye = (row == column).astype(F32)
    gram = system_ref[...]
    rho = jnp.sum(gram * eye) / K
    system = gram + rho * eye
    row_sums = jnp.sum(jnp.abs(system), axis=1, keepdims=True)
    bound = jnp.minimum(jnp.max(row_sums), (K + 1) * rho)
    inverse[...] = eye * (2.0 / (bound + rho))
    parts = split(system)

    def step(index, carry):
        value = inverse[...]
        pieces = split(value)
        residual = 2.0 * eye - dot_split(parts, pieces)
        inverse[...] = dot_split(pieces, split(residual))
        return carry

    lax.fori_loop(0, INVERSE_STEPS, step, 0)


def solve_kernel(
    n, mp, width, share, rows, weights_ref, system_ref, slice_ref, gradient_ref,
    merged_ref, solved_ref, grad, level, inverse, proj, sums, mp_slots,
    local_sem, s0, r0, s1, r1, s2, r2, s3, r3,
):
    me_dp, me_mp = lax.axis_index("dp"), lax.axis_index("mp")
    load = pltpu.make_async_copy(gradient_ref, grad, local_sem)
    load.start()
    mine = merged_ref.at[:, columns_of(me_dp, width)]
    source, first, blocks = slice_ref, 0, n
    while blocks > 1:
        blocks //= 2
        for p in range(blocks):
            value = dot(weights_ref[first + p], source[2 * K * p:2 * K * (p + 1), :]).astype(BF16)
            if blocks == 1:
                mine[...] = value
            else:
                level[p * K:(p + 1) * K, :] = value
        source = level
        first += blocks
    greet(("dp", "mp"))
    def pass_on(index, offset, semaphores):
        part = merged_ref.at[:, columns_of(index, width)]
        at = lax.rem(index + n, n)
        return pltpu.make_async_remote_copy(
            src_ref=part,
            dst_ref=part,
            send_sem=semaphores[0].at[at],
            recv_sem=semaphores[1].at[at],
            device_id={"dp": lax.rem(me_dp + offset + n, n)},
            device_id_type=MESH,
        )

    up, down = (s0, r0), (s3, r3)

    @pl.when(me_dp < n - 1)
    def _():
        pass_on(me_dp, 1, up).start()

    @pl.when(me_dp > 0)
    def _():
        pass_on(me_dp, -1, down).start()

    invert(system_ref, inverse)
    load.wait()
    tile = rows // 4

    def multiply(index, start):
        def body(t, carry):
            at = rows_of(t, tile)
            value = dot(
                grad[at, columns_of(index, width)], merged_ref[:, columns_of(index, width)], NT
            )
            sums[at, :] = value if start else sums[at, :] + value
            return carry

        lax.fori_loop(0, 4, body, 0)

    multiply(me_dp, True)
    for d in range(1, n):
        below, above = me_dp - d, me_dp + d

        @pl.when(below >= 0)
        def _():
            pass_on(below, 1, up).wait_recv()

        @pl.when((below >= 0) & (me_dp < n - 1))
        def _():
            pass_on(below, 1, up).start()

        @pl.when(above < n)
        def _():
            pass_on(above, -1, down).wait_recv()

        @pl.when((above < n) & (me_dp > 0))
        def _():
            pass_on(above, -1, down).start()

        @pl.when(below >= 0)
        def _():
            multiply(below, False)

        @pl.when(above < n)
        def _():
            multiply(above, False)

    for d in range(n):

        @pl.when((me_dp - d >= 0) & (me_dp < n - 1))
        def _():
            pass_on(me_dp - d, 1, up).wait_send()

        @pl.when((me_dp + d < n) & (me_dp > 0))
        def _():
            pass_on(me_dp + d, -1, down).wait_send()

    proj[:rows, :] = sums[...].astype(BF16)
    if share * mp > rows:
        proj[rows:, :] = jnp.zeros((share * mp - rows, K), BF16)
    copies = [
        send("mp", d, proj.at[rows_of(peer("mp", d), share)], mp_slots.at[me_mp], s1, r1)
        for d in range(1, mp)
    ]
    mp_slots[me_mp] = proj[rows_of(me_mp, share), :]
    for copy in copies:
        copy.wait()
    solved = dot_split(split(sum_slots(mp_slots)), split(inverse[...]))
    part = solved_ref.at[rows_of(me_mp, share)]
    part[...] = solved.astype(BF16)
    copies = [send("mp", d, part, part, s2, r2) for d in range(1, mp)]
    for copy in copies:
        copy.wait()


def subtract_kernel(gradient_ref, solved_ref, merged_ref, result_ref):
    result = gradient_ref[...].astype(F32) - dot(solved_ref[...], merged_ref[...])
    result_ref[...] = result.astype(BF16)


def vmem():
    return pl.BlockSpec(memory_space=pltpu.VMEM)


def anywhere():
    return pl.BlockSpec(memory_space=pl.ANY)


def dma(count):
    return pltpu.SemaphoreType.DMA((count,))


def round_up(value, multiple):
    return -(-value // multiple) * multiple


def local(gradient, sketches, start_basis):
    n, mp = lax.axis_size("dp"), lax.axis_size("mp")
    rows, columns = gradient.shape
    width = round_up(-(-columns // n), 128)
    padding = ((0, 0), (0, width * n - columns))
    wide_gradient, wide_sketches = gradient, sketches
    if width * n > columns:
        wide_gradient, wide_sketches = jnp.pad(gradient, padding), jnp.pad(sketches, padding)

    gram_rows = n * (n + 1) // 2 * K
    share = round_up(-(-gram_rows // mp), 16 * n)
    gram_rows = share * mp
    one = pltpu.SemaphoreType.DMA
    slices, gram, turned = pl.pallas_call(
        functools.partial(gram_kernel, n, mp, width, share),
        out_shape=[
            jax.ShapeDtypeStruct((n * K, width), BF16),
            jax.ShapeDtypeStruct((gram_rows, K), BF16),
            jax.ShapeDtypeStruct((K, 2 * K), F32),
        ],
        in_specs=[anywhere(), vmem()],
        out_specs=[vmem(), vmem(), vmem()],
        scratch_shapes=[
            pltpu.VMEM((gram_rows, K), BF16),
            pltpu.VMEM((gram_rows // 2, K), BF16),
            pltpu.VMEM((gram_rows // 2, K), BF16),
            pltpu.VMEM((mp // 2, share, K), BF16),
            pltpu.VMEM((share, K), BF16),
            pltpu.VMEM((n, share // n, K), BF16),
            one, dma(n - 1), dma(n - 1), one, one, dma(mp // 2 - 1), dma(mp // 2 - 1),
            dma(n - 1), dma(n - 1), dma(mp // 2 - 1), dma(mp // 2 - 1), one, one,
            dma(n - 1), dma(n - 1),
        ],
        compiler_params=pltpu.CompilerParams(
            collective_id=0, has_side_effects=True, vmem_limit_bytes=MIB * 16 + 8 * gram_rows * K
        ),
        cost_estimate=pl.CostEstimate(
            flops=60 * 10**9, bytes_accessed=2 * 10**8, transcendentals=0
        ),
        name="gram",
    )(wide_sketches, start_basis)

    weights, system = pl.pallas_call(
        functools.partial(merge_kernel, n),
        out_shape=[
            jax.ShapeDtypeStruct((n - 1, K, 2 * K), BF16),
            jax.ShapeDtypeStruct((K, K), F32),
        ],
        in_specs=[vmem(), vmem()],
        out_specs=[vmem(), vmem()],
        scratch_shapes=[
            pltpu.VMEM((n * K, n * K), F32),
            pltpu.VMEM((n * K // 2, n * K // 2), F32),
            pltpu.VMEM((n // 2, K, 2 * K), F32),
            pltpu.VMEM((n, 2 * K, 2 * K), BF16),
        ],
        compiler_params=pltpu.CompilerParams(vmem_limit_bytes=MIB * 16 + 8 * (n * K) ** 2),
        cost_estimate=pl.CostEstimate(
            flops=40 * 10**9, bytes_accessed=10**8, transcendentals=0
        ),
        name="merge",
    )(gram, turned)

    share = round_up(-(-rows // mp), 16)
    merged, solved = pl.pallas_call(
        functools.partial(solve_kernel, n, mp, width, share, rows),
        out_shape=[
            jax.ShapeDtypeStruct((K, n * width), BF16),
            jax.ShapeDtypeStruct((share * mp, K), BF16),
        ],
        in_specs=[vmem(), vmem(), vmem(), anywhere()],
        out_specs=[vmem(), vmem()],
        scratch_shapes=[
            pltpu.VMEM((rows, n * width), BF16),
            pltpu.VMEM((n // 2 * K, width), BF16),
            pltpu.VMEM((K, K), F32),
            pltpu.VMEM((share * mp, K), BF16),
            pltpu.VMEM((rows, K), F32),
            pltpu.VMEM((mp, share, K), BF16),
            one, dma(n), dma(n), dma(mp - 1), dma(mp - 1), dma(mp - 1), dma(mp - 1), dma(n), dma(n),
        ],
        compiler_params=pltpu.CompilerParams(
            collective_id=1, has_side_effects=True, vmem_limit_bytes=MIB * 20 + 2 * rows * n * width
        ),
        name="solve",
    )(weights, system, slices, wide_gradient)
    tile = rows // 8 if rows % 128 == 0 else rows
    return pl.pallas_call(
        subtract_kernel,
        out_shape=jax.ShapeDtypeStruct((rows, columns), BF16),
        grid=(rows // tile,),
        in_specs=[
            pl.BlockSpec((tile, columns), lambda i: (i, 0)),
            pl.BlockSpec((tile, K), lambda i: (i, 0)),
            pl.BlockSpec((K, columns), lambda i: (0, 0)),
        ],
        out_specs=pl.BlockSpec((tile, columns), lambda i: (i, 0)),
        compiler_params=pltpu.CompilerParams(vmem_limit_bytes=MIB * 24),
        name="subtract",
    )(gradient, solved[:rows], merged[:, :columns])


def solution(mesh):
    in_specs = (P("dp", "mp"), P("dp", "mp"), P())
    out_specs = P("dp", "mp")
    return jax.shard_map(local, mesh=mesh, in_specs=in_specs, out_specs=out_specs, check_vma=False)
```
